32 devices in a mesh: fsdp: 4 (over x, core), owner: 8 (over z, y).
Axes of the slice: x: 2, y: 2, z: 4, core: 2. Of those that a mesh axis runs over, the one named last changes fastest.
Arguments:
- grads: bfloat16 [16, 2560, 5120], P('owner', 'fsdp'), may hold values from -6 to 6
- assign: int32 [160, 1], replicated, may hold values from 0 to 7; in each aligned block of 20 rows (0 to 19, 20 to 39, ...) at most 4 rows name the same one
- bases: bfloat16 [8, 32, 512, 512], P('owner', None, 'fsdp'), may hold values from -0.25 to 0.25
- eigvals: bfloat16 [8, 32, 512], P('owner'), may hold values from 0.099609375 to 10
Outputs:
- update: bfloat16 [16, 2560, 5120], P('owner', 'fsdp')
The draws below stay inside these ranges and needn't reach their ends.
Inputs may be any that keep to these rules, and one draw needn't show every extreme that they name: `assign`: within each aligned block of 20 units (the matrices of one index of owner) no owner is named more than 4 times; in some block one owner is named exactly 4 times.
All inputs are finite; a program needn't handle non-finite values.
Results may differ from the reference program's by a relative error of at most 0.0043.
Values may be sent and summed in bfloat16 or wider, within the bound.
A program may use at most 128 MiB of HBM per device.

```python
import math
import jax
import jax.numpy as jnp
import numpy as np
from jax import lax

C = 5120
R = 2560
BLK = 512
NBLK = 10
MATS = 16
UNITS_SRC = 20
UNITS = 160
PEER_CAP = 4
SLOTS = 32
N_OWNER = 8


def block_scale(own_key, dims, cuts, low, top_value):
    def one(dim, blocks):
        heights = jax.random.uniform(jax.random.fold_in(jax.random.fold_in(own_key, 6), dim), (blocks,), jnp.float32, low / len(cuts), top_value / len(cuts))
        return jnp.repeat(jnp.exp(heights), dims[dim] // blocks).reshape((-1,) + (1,) * (len(dims) - dim - 1))

    loudness = one(*cuts[0])
    for cut in cuts[1:]:
        loudness = loudness * one(*cut)
    return loudness


def assign_block(own_key, own, number, rows, count, top, reach, lean):
    ranking = jax.random.permutation(own_key, count)
    crowded, ordinary = shares(count, rows * top, reach, lean, True), shares(count, rows * top, reach, lean, False)
    places = jnp.arange(count)

    def named(sizes, offset_by):
        used = int((sizes > 0).sum())
        fixed = max(1, used // 4)
        shifted = fixed + (places - fixed + offset_by * (used - fixed)) % max(1, count - fixed)
        return jnp.zeros((count,), jnp.int32).at[ranking[jnp.where(places < fixed, places, shifted)]].set(jnp.asarray(sizes, jnp.int32))

    sizes = jnp.where(number % 4 == 0, named(crowded, number // 4), named(ordinary, number - number // 4 - 1))
    mixed = jax.random.permutation(jax.random.fold_in(own, 3), count)
    giver, sink = mixed[0:count // 2 * 2:2], mixed[1:count // 2 * 2:2]
    slack = jnp.minimum(sizes[giver] - 1, reach - sizes[sink]) // 2
    slack = jnp.where((giver == ranking[0]) | (sink == ranking[0]) | (sizes[sink] == 0), 0, jnp.maximum(slack, 0))
    shifted = jax.random.randint(jax.random.fold_in(own, 4), (count // 2,), 0, 1 << 20) % (slack + 1)
    sizes = sizes.at[giver].add(-shifted).at[sink].add(shifted)
    items = jnp.searchsorted(jnp.cumsum(sizes), jnp.arange(rows * top), side="right").astype(jnp.int32)
    listing = items.reshape(top, rows).T
    listing = listing[jax.random.permutation(jax.random.fold_in(own, 1), rows)]
    offset_by = jax.random.randint(jax.random.fold_in(own, 2), (rows, 1), 0, top)
    return jnp.take_along_axis(listing, (jnp.arange(top)[None, :] + offset_by) % top, axis=1)


def shares(count, total, most, slope, full):
    weights = [(1 << 20) // math.isqrt(standing ** slope) + 1 for standing in range(1, count + 1)]
    largest = most if full else min(most, max(-(-total // count), total * weights[0] // sum(weights)))
    least = 1 if total - largest >= count - 1 else 0
    holding, surplus = [largest] + [least] * (count - 1), total - largest - least * (count - 1)
    while surplus > 0:
        movable = [i for i in range(1, count) if holding[i] < largest] or [i for i in range(1, count) if holding[i] < most]
        mass, remaining = sum([weights[i] for i in movable]), surplus
        for i in movable:
            more = min(most - holding[i], max(1, remaining * weights[i] // mass), surplus)
            holding[i] = holding[i] + more
            surplus = surplus - more
    return np.array(holding)


def normal_values(own_key, extent, scale, bound, cuts=(), kind=jnp.bfloat16):
    loudness = block_scale(own_key, extent, cuts, -0.22, 0.18) if cuts else 1.0
    drawn = jax.random.normal(own_key, extent, jnp.float32) * scale * loudness
    return jnp.minimum(jnp.maximum(drawn, -bound), bound).astype(kind)


def setup_inputs(seed: int = 0) -> dict:
    key_of = jax.random.split(jax.random.key(seed), 5)
    grads = normal_values(key_of[0], (MATS, R, C), 1.0, 6.0, ((0, 8), (1, 4)))
    assign_keys = jax.random.split(jax.random.fold_in(key_of[1], 1), UNITS // UNITS_SRC)
    assign_turns = jax.random.permutation(jax.random.fold_in(key_of[1], 3), UNITS // UNITS_SRC)
    assign = jax.vmap(lambda own, number: assign_block(jax.random.fold_in(key_of[1], 2), own, number, UNITS_SRC, N_OWNER, 1, PEER_CAP, 2))(assign_keys, assign_turns).reshape((UNITS, 1))
    bases = normal_values(key_of[2], (N_OWNER, SLOTS, BLK, BLK), BLK ** -0.5, 0.25, ((0, 8), (2, 4)))
    eigvals = jnp.clip(jnp.exp(math.log(10.0) - 4.609084 * jax.random.uniform(key_of[3], (N_OWNER, SLOTS, BLK), jnp.float32) ** block_scale(key_of[3], (N_OWNER, SLOTS, BLK), ((0, 8),), -0.2, 0.2)), 0.099609375, 10.0).astype(jnp.bfloat16)
    return dict(grads=grads, assign=assign, bases=bases, eigvals=eigvals)


DAMPING = 0.1


def reference(grads, assign, bases, eigvals):
    owner_table = assign[:, 0].reshape(N_OWNER, UNITS_SRC)
    owner_ids = jnp.arange(N_OWNER, dtype=jnp.int32)
    owner_hits = (owner_table[:, :, None] == owner_ids[None, None, :]).astype(jnp.int32)
    slot_ranks = jnp.sum((jnp.cumsum(owner_hits, axis=1) - 1) * owner_hits, axis=2).astype(jnp.int32)
    sources = jnp.arange(N_OWNER, dtype=jnp.int32)[:, None] * jnp.ones((1, UNITS_SRC), jnp.int32)
    slot_ids = (sources * PEER_CAP + slot_ranks).reshape(-1).astype(jnp.int32)
    owner_flat = owner_table.reshape(-1).astype(jnp.int32)
    panels = grads.reshape(MATS, R, NBLK, BLK).transpose(0, 2, 1, 3).reshape(UNITS, R, BLK)

    def one_unit(items):
        panel_block, owner_id, slot_id = items
        basis_block = bases[owner_id, slot_id]
        eigen_vals = eigvals[owner_id, slot_id].astype(jnp.float32)
        turned = jnp.dot(panel_block, basis_block, preferred_element_type=jnp.float32)
        scaled = (turned / (eigen_vals[None, :] + DAMPING)).astype(jnp.bfloat16)
        return jnp.dot(scaled, basis_block.T, preferred_element_type=jnp.float32).astype(jnp.bfloat16)

    result = lax.map(one_unit, (panels, owner_flat, slot_ids))
    return result.reshape(MATS, NBLK, R, BLK).transpose(0, 2, 1, 3).reshape(MATS, R, C)
```

```python
import functools
import jax
import jax.numpy as jnp
from jax import lax
from jax.experimental import pallas as pl
from jax.experimental.pallas import tpu as pltpu
from jax.sharding import PartitionSpec as P

BLK = 512
DAMPING = 0.1


def rotate_kernel(first, kinds, unit_ref, rank_ref, owner_ref, *refs):
    panel_ref, inverse_ref = refs[0], refs[1]
    basis_refs, out_ref = refs[2 : 2 + kinds], refs[-1]
    rank = rank_ref[first + pl.program_id(0)]
    for kind in range(kinds):

        @pl.when(rank == kind)
        def _():
            basis = basis_refs[kind][0]
            turned = jnp.dot(panel_ref[0], basis, preferred_element_type=jnp.float32)
            scaled = (turned * inverse_ref[0]).astype(jnp.bfloat16)
            out_ref[0] = lax.dot_general(
                scaled, basis, (((1,), (1,)), ((), ())), preferred_element_type=jnp.float32
            ).astype(jnp.bfloat16)


def rotate(first, count, blocks, last_packed, scalars, grads, inverse, bases, so_far):
    row_count = grads.shape[1]
    kinds = len(bases)

    def panel_map(i, unit, rank, owner):
        u = unit[first + i]
        return u // blocks, 0, u % blocks

    def inverse_map(i, unit, rank, owner):
        return first + i, 0, 0

    def basis_map(kind, i, unit, rank, owner):
        place = i if last_packed and kind == kinds - 1 else owner[first + i]
        return jnp.where(rank[first + i] == kind, place, 0), 0, 0

    in_specs = [
        pl.BlockSpec((1, row_count, BLK), panel_map),
        pl.BlockSpec((1, 1, BLK), inverse_map),
    ] + [pl.BlockSpec((1, BLK, BLK), functools.partial(basis_map, kind)) for kind in range(kinds)]
    operands = [grads, inverse, *bases]
    aliases = {}
    if so_far is not None:
        in_specs.append(pl.BlockSpec(memory_space=pl.ANY))
        aliases = {len(scalars) + len(operands): 0}
        operands.append(so_far)
    return pl.pallas_call(
        functools.partial(rotate_kernel, first, kinds),
        grid_spec=pltpu.PrefetchScalarGridSpec(
            num_scalar_prefetch=len(scalars),
            grid=(count,),
            in_specs=in_specs,
            out_specs=pl.BlockSpec((1, row_count, BLK), panel_map),
        ),
        out_shape=jax.ShapeDtypeStruct(grads.shape, grads.dtype),
        input_output_aliases=aliases,
        compiler_params=pltpu.CompilerParams(vmem_limit_bytes=60 * 1024 * 1024),
        cost_estimate=pl.CostEstimate(
            flops=count * 4 * row_count * BLK * BLK,
            bytes_accessed=count * (4 * row_count * BLK + 2 * BLK * BLK),
            transcendentals=0,
        ),
        name="rotate",
    )(*scalars, *operands)


def per_device(grads, assign, bases, eigvals):
    owner_count = lax.axis_size("owner")
    owner_here = lax.axis_index("owner")
    matrices, row_count, col_count = grads.shape
    block_count = col_count // BLK
    unit_count = matrices * block_count
    slot_count = bases.shape[1]
    per_peer = slot_count // owner_count

    all_eigen = lax.all_gather(eigvals[0], "owner", axis=0, tiled=False)

    units = jnp.arange(unit_count, dtype=jnp.int32)
    owners = lax.dynamic_slice_in_dim(assign[:, 0], owner_here * unit_count, unit_count)
    earlier = units[None, :] < units[:, None]
    ranks = jnp.sum((owners[None, :] == owners[:, None]) & earlier, axis=1, dtype=jnp.int32)
    before = (ranks[None, :] < ranks[:, None]) | ((ranks[None, :] == ranks[:, None]) & earlier)
    places = jnp.sum(before, axis=1, dtype=jnp.int32)
    code = (ranks * owner_count + owners) * unit_count + units
    code = jnp.sum(jnp.where(places[None, :] == units[:, None], code[None, :], 0), axis=1, dtype=jnp.int32)
    unit_at = code % unit_count
    owner_at = code // unit_count % owner_count
    rank_at = code // (unit_count * owner_count)
    scalars = (unit_at, rank_at, owner_at)

    tail = unit_count // per_peer
    head = unit_count - tail
    local = bases[0].reshape((owner_count, per_peer) + bases.shape[2:])
    full = []
    for rank in range(per_peer):
        moved = lax.all_to_all(local[:, rank], "owner", split_axis=0, concat_axis=0, tiled=True)
        if rank == per_peer - 1:
            moved = moved[owner_at[head:]]
        full.append(lax.all_gather(moved, "fsdp", axis=1, tiled=True))

    eigen = all_eigen[owner_at, owner_here * per_peer + rank_at]
    inverse = (1.0 / (eigen.astype(jnp.float32) + DAMPING))[:, None, :]
    out = rotate(0, head, block_count, False, scalars, grads, inverse, full[:-1], None)
    return rotate(head, tail, block_count, True, scalars, grads, inverse, full, out)


def solution(mesh):
    in_specs = (
        P("owner", "fsdp", None),
        P(),
        P("owner", None, "fsdp", None),
        P("owner", None, None),
    )
    out_specs = P("owner", "fsdp", None)
    return jax.shard_map(
        per_device, mesh=mesh, in_specs=in_specs, out_specs=out_specs, check_vma=False
    )
```

```python
import functools
import jax
import jax.numpy as jnp
from jax import lax
from jax.experimental import pallas as pl
from jax.experimental.pallas import tpu as pltpu
from jax.sharding import PartitionSpec as P

BLK = 512
DAMPING = 0.1
STRIDE = 5
LAG = 4
MESH = pl.DeviceIdType.MESH
VMEM_LIMIT = 60 * 1024 * 1024


def gather_kernel(
    owners, shards, per_peer,
    bases_ref, inverse_ref, full_ref, full_inverse_ref,
    own_sem, own_inverse_sem, move_send, move_recv, inverse_send, inverse_recv,
    row_send, row_recv, core_send, core_recv,
):
    me, shard = lax.axis_index("owner"), lax.axis_index("fsdp")
    chips = shards // 2
    chip, core = shard // 2, shard % 2
    sibling = chip * 2 + (1 - core)
    pieces = owners * per_peer

    def to(dst_shard, dst_owner):
        return (dst_shard, dst_owner)

    barrier = pltpu.get_barrier_semaphore()
    for step in range(1, owners):
        pl.semaphore_signal(barrier, inc=1, device_id=to(shard, (me + step) % owners), device_id_type=MESH)
    for step in range(1, chips):
        pl.semaphore_signal(barrier, inc=1, device_id=to((chip + step) % chips * 2 + core, me), device_id_type=MESH)
    pl.semaphore_signal(barrier, inc=1, device_id=to(sibling, me), device_id_type=MESH)
    pl.semaphore_wait(barrier, owners - 1 + chips)

    def place(index):
        return index // owners, index % owners

    def move(index):
        rank, turn = place(index)
        target = (me + turn * STRIDE) % owners
        return pltpu.make_async_remote_copy(
            src_ref=bases_ref.at[target, rank],
            dst_ref=full_ref.at[me, rank, shard],
            send_sem=move_send.at[index],
            recv_sem=move_recv.at[index],
            device_id=to(shard, target),
            device_id_type=MESH,
        )

    def move_inverse(turn):
        target = (me + turn * STRIDE) % owners
        return pltpu.make_async_remote_copy(
            src_ref=inverse_ref.at[target],
            dst_ref=full_inverse_ref.at[me],
            send_sem=inverse_send.at[turn],
            recv_sem=inverse_recv.at[turn],
            device_id=to(shard, target),
            device_id_type=MESH,
        )

    def piece(index, shard_of):
        rank, turn = place(index)
        source = (me + owners * STRIDE - turn * STRIDE) % owners
        return full_ref.at[source, rank, shard_of]

    def along_x(index, step):
        ref = piece(index, shard)
        return pltpu.make_async_remote_copy(
            src_ref=ref, dst_ref=ref,
            send_sem=row_send.at[step - 1, index],
            recv_sem=row_recv.at[step - 1, index],
            device_id=to((chip + step) % chips * 2 + core, me),
            device_id_type=MESH,
        )

    def across(index, step):
        ref = piece(index, (chip + chips - step) % chips * 2 + core)
        return pltpu.make_async_remote_copy(
            src_ref=ref, dst_ref=ref,
            send_sem=core_send.at[step, index],
            recv_sem=core_recv.at[step, index],
            device_id=to(sibling, me),
            device_id_type=MESH,
        )

    def own(rank):
        return pltpu.make_async_copy(bases_ref.at[me, rank], full_ref.at[me, rank, shard], own_sem.at[rank])

    own_inverse = pltpu.make_async_copy(inverse_ref.at[me], full_inverse_ref.at[me], own_inverse_sem)

    for rank in range(per_peer):
        own(rank).start()

    @pl.loop(0, pieces)
    def _(index):
        @pl.when(index % owners > 0)
        def _():
            move(index).start()

    own_inverse.start()

    @pl.loop(1, owners)
    def _(turn):
        move_inverse(turn).start()

    for rank in range(per_peer):
        own(rank).wait()

    def pass_on(index):
        for step in range(1, chips):
            along_x(index, step).wait_recv()
            across(index, step).start()

    @pl.loop(0, pieces)
    def _(index):
        @pl.when(index % owners > 0)
        def _():
            move(index).wait_recv()

        for step in range(1, chips):
            along_x(index, step).start()
        across(index, 0).start()

        @pl.when(index >= LAG)
        def _():
            pass_on(index - LAG)

    @pl.loop(pieces - LAG, pieces)
    def _(index):
        pass_on(index)

    own_inverse.wait()

    @pl.loop(1, owners)
    def _(turn):
        move_inverse(turn).wait()

    @pl.loop(0, pieces)
    def _(index):
        @pl.when(index % owners > 0)
        def _():
            move(index).wait_send()

        for step in range(1, chips):
            along_x(index, step).wait_send()
        for step in range(chips):
            across(index, step).wait()


def gather(bases, inverse):
    owners, shards = lax.axis_size("owner"), lax.axis_size("fsdp")
    per_peer = bases.shape[1]
    pieces, chips = owners * per_peer, shards // 2
    dma = pltpu.SemaphoreType.DMA
    anywhere = pl.BlockSpec(memory_space=pl.ANY)
    return pl.pallas_call(
        functools.partial(gather_kernel, owners, shards, per_peer),
        out_shape=(
            jax.ShapeDtypeStruct(bases.shape[:2] + (shards,) + bases.shape[2:], bases.dtype),
            jax.ShapeDtypeStruct(inverse.shape, inverse.dtype),
        ),
        in_specs=[anywhere, anywhere],
        out_specs=(anywhere, anywhere),
        scratch_shapes=[
            dma((per_peer,)), dma,
            dma((pieces,)), dma((pieces,)),
            dma((owners,)), dma((owners,)),
            dma((chips - 1, pieces)), dma((chips - 1, pieces)),
            dma((chips, pieces)), dma((chips, pieces)),
        ],
        compiler_params=pltpu.CompilerParams(
            collective_id=0, has_side_effects=True, vmem_limit_bytes=VMEM_LIMIT
        ),
        name="gather",
    )(bases, inverse)


def rotate_kernel(group, slot_ref, panel_ref, *refs):
    inverse_refs, basis_refs, out_ref = refs[:group], refs[group : 2 * group], refs[-1]
    for at in range(group):
        columns = slice(at * BLK, (at + 1) * BLK)
        basis = basis_refs[at][0]
        turned = jnp.dot(panel_ref[0, :, columns], basis, preferred_element_type=jnp.float32)
        scaled = (turned * inverse_refs[at][0]).astype(jnp.bfloat16)
        out_ref[0, :, columns] = lax.dot_general(
            scaled, basis, (((1,), (1,)), ((), ())), preferred_element_type=jnp.float32
        ).astype(jnp.bfloat16)


def rotate(slots, grads, inverse, bases):
    matrices, row_count, col_count = grads.shape
    block_count = col_count // BLK
    group = 2 if block_count % 2 == 0 else 1
    steps = block_count // group

    def panel_map(i, slot):
        return i // steps, 0, i % steps

    def slot_map(at, i, slot):
        return slot[i * group + at], 0, 0

    panel = pl.BlockSpec((1, row_count, group * BLK), panel_map)
    return pl.pallas_call(
        functools.partial(rotate_kernel, group),
        grid_spec=pltpu.PrefetchScalarGridSpec(
            num_scalar_prefetch=1,
            grid=(matrices * steps,),
            in_specs=[panel]
            + [pl.BlockSpec((1, 1, BLK), functools.partial(slot_map, at)) for at in range(group)]
            + [pl.BlockSpec((1, BLK, BLK), functools.partial(slot_map, at)) for at in range(group)],
            out_specs=panel,
        ),
        out_shape=jax.ShapeDtypeStruct(grads.shape, grads.dtype),
        compiler_params=pltpu.CompilerParams(vmem_limit_bytes=VMEM_LIMIT),
        cost_estimate=pl.CostEstimate(
            flops=4 * matrices * row_count * col_count * BLK,
            bytes_accessed=4 * matrices * row_count * col_count + 2 * matrices * col_count * BLK,
            transcendentals=0,
        ),
        name="rotate",
    )(slots, grads, *[inverse] * group, *[bases] * group)


def per_device(grads, assign, bases, eigvals):
    owner_count = lax.axis_size("owner")
    owner_here = lax.axis_index("owner")
    matrices, _, col_count = grads.shape
    unit_count = matrices * col_count // BLK
    slot_count = bases.shape[1]
    per_peer = slot_count // owner_count

    units = jnp.arange(unit_count, dtype=jnp.int32)
    owners = lax.dynamic_slice_in_dim(assign[:, 0], owner_here * unit_count, unit_count)
    earlier = units[None, :] < units[:, None]
    ranks = jnp.sum((owners[None, :] == owners[:, None]) & earlier, axis=1, dtype=jnp.int32)
    slots = owners * per_peer + ranks

    inverse = 1.0 / (eigvals[0].astype(jnp.float32) + DAMPING)
    full, full_inverse = gather(
        bases[0].reshape((owner_count, per_peer) + bases.shape[2:]),
        inverse.reshape(owner_count, per_peer, 1, BLK),
    )
    return rotate(
        slots, grads, full_inverse.reshape(slot_count, 1, BLK), full.reshape(slot_count, BLK, BLK)
    )


def solution(mesh):
    in_specs = (
        P("owner", "fsdp", None),
        P(),
        P("owner", None, "fsdp", None),
        P("owner", None, None),
    )
    out_specs = P("owner", "fsdp", None)
    return jax.shard_map(
        per_device, mesh=mesh, in_specs=in_specs, out_specs=out_specs, check_vma=False
    )
```

```python
import functools
import jax
import jax.numpy as jnp
from jax import lax
from jax.experimental import pallas as pl
from jax.experimental.pallas import tpu as pltpu
from jax.sharding import PartitionSpec as P

BLK = 512
DAMPING = 0.1
LAG = 4
WINDOW = 6
MESH = pl.DeviceIdType.MESH
VMEM_LIMIT = 60 * 1024 * 1024


def gather_kernel(
    owners, shards, per_peer,
    bases_ref, inverse_ref, full_ref, full_inverse_ref,
    own_sem, own_inverse_sem, move_send, move_recv, inverse_send, inverse_recv,
    row_send, row_recv, core_send, core_recv,
):
    me, shard = lax.axis_index("owner"), lax.axis_index("fsdp")
    chips = shards // 2
    chip, core = shard // 2, shard % 2
    sibling = chip * 2 + (1 - core)
    pieces = owners * per_peer

    def to(dst_shard, dst_owner):
        return (dst_shard, dst_owner)

    barrier = pltpu.get_barrier_semaphore()
    for step in range(1, owners):
        pl.semaphore_signal(barrier, inc=1, device_id=to(shard, (me + step) % owners), device_id_type=MESH)
    for step in range(1, chips):
        pl.semaphore_signal(barrier, inc=1, device_id=to((chip + step) % chips * 2 + core, me), device_id_type=MESH)
    pl.semaphore_signal(barrier, inc=1, device_id=to(sibling, me), device_id_type=MESH)
    pl.semaphore_wait(barrier, owners - 1 + chips)

    def place(index):
        return index // owners, index % owners

    def partner(turn):
        across_bits = turn % 2 * (owners // 2) + turn // 2
        other, bit = 0, 1
        while bit < owners:
            other = other + (me // bit % 2 + across_bits // bit % 2) % 2 * bit
            bit *= 2
        return other

    def move(index):
        rank, turn = place(index)
        target = partner(turn)
        return pltpu.make_async_remote_copy(
            src_ref=bases_ref.at[target, rank],
            dst_ref=full_ref.at[me, rank, shard],
            send_sem=move_send.at[index],
            recv_sem=move_recv.at[index],
            device_id=to(shard, target),
            device_id_type=MESH,
        )

    def move_inverse(turn):
        target = partner(turn)
        return pltpu.make_async_remote_copy(
            src_ref=inverse_ref.at[target],
            dst_ref=full_inverse_ref.at[me],
            send_sem=inverse_send.at[turn],
            recv_sem=inverse_recv.at[turn],
            device_id=to(shard, target),
            device_id_type=MESH,
        )

    def piece(index, shard_of):
        rank, turn = place(index)
        return full_ref.at[partner(turn), rank, shard_of]

    def along_x(index, step):
        ref = piece(index, shard)
        return pltpu.make_async_remote_copy(
            src_ref=ref, dst_ref=ref,
            send_sem=row_send.at[step - 1, index],
            recv_sem=row_recv.at[step - 1, index],
            device_id=to((chip + step) % chips * 2 + core, me),
            device_id_type=MESH,
        )

    def across(index, step):
        ref = piece(index, (chip + chips - step) % chips * 2 + core)
        return pltpu.make_async_remote_copy(
            src_ref=ref, dst_ref=ref,
            send_sem=core_send.at[step, index],
            recv_sem=core_recv.at[step, index],
            device_id=to(sibling, me),
            device_id_type=MESH,
        )

    def own(rank):
        return pltpu.make_async_copy(bases_ref.at[me, rank], full_ref.at[me, rank, shard], own_sem.at[rank])

    own_inverse = pltpu.make_async_copy(inverse_ref.at[me], full_inverse_ref.at[me], own_inverse_sem)

    for rank in range(per_peer):
        own(rank).start()

    @pl.loop(1, 1 + WINDOW)
    def _(index):
        move(index).start()

    own_inverse.start()

    @pl.loop(1, owners)
    def _(turn):
        move_inverse(turn).start()

    for rank in range(per_peer):
        own(rank).wait()

    def pass_on(index):
        for step in range(1, chips):
            along_x(index, step).wait_recv()
            across(index, step).start()

    @pl.loop(0, pieces)
    def _(index):
        @pl.when(index % owners > 0)
        def _():
            move(index).wait_recv()

        for step in range(1, chips):
            along_x(index, step).start()
        across(index, 0).start()
        later = index + 1 + WINDOW

        @pl.when((later < pieces) & (later % owners > 0))
        def _():
            move(later).start()

        @pl.when(index >= LAG)
        def _():
            pass_on(index - LAG)

    @pl.loop(pieces - LAG, pieces)
    def _(index):
        pass_on(index)

    own_inverse.wait()

    @pl.loop(1, owners)
    def _(turn):
        move_inverse(turn).wait()

    @pl.loop(0, pieces)
    def _(index):
        @pl.when(index % owners > 0)
        def _():
            move(index).wait_send()

        for step in range(1, chips):
            along_x(index, step).wait_send()
        for step in range(chips):
            across(index, step).wait()


def gather(bases, inverse):
    owners, shards = lax.axis_size("owner"), lax.axis_size("fsdp")
    per_peer = bases.shape[1]
    pieces, chips = owners * per_peer, shards // 2
    dma = pltpu.SemaphoreType.DMA
    anywhere = pl.BlockSpec(memory_space=pl.ANY)
    return pl.pallas_call(
        functools.partial(gather_kernel, owners, shards, per_peer),
        out_shape=(
            jax.ShapeDtypeStruct(bases.shape[:2] + (shards,) + bases.shape[2:], bases.dtype),
            jax.ShapeDtypeStruct(inverse.shape, inverse.dtype),
        ),
        in_specs=[anywhere, anywhere],
        out_specs=(anywhere, anywhere),
        scratch_shapes=[
            dma((per_peer,)), dma,
            dma((pieces,)), dma((pieces,)),
            dma((owners,)), dma((owners,)),
            dma((chips - 1, pieces)), dma((chips - 1, pieces)),
            dma((chips, pieces)), dma((chips, pieces)),
        ],
        compiler_params=pltpu.CompilerParams(
            collective_id=0, has_side_effects=True, vmem_limit_bytes=VMEM_LIMIT
        ),
        name="gather",
    )(bases, inverse)


def rotate_kernel(group, slot_ref, panel_ref, *refs):
    inverse_refs, basis_refs, out_ref = refs[:group], refs[group : 2 * group], refs[-1]
    scaled = []
    for at in range(group):
        panel = panel_ref[0, :, at * BLK : (at + 1) * BLK]
        turned = jnp.dot(panel, basis_refs[at][0], preferred_element_type=jnp.float32)
        scaled.append((turned * inverse_refs[at][0]).astype(jnp.bfloat16))
    for at in range(group):
        out_ref[0, :, at * BLK : (at + 1) * BLK] = lax.dot_general(
            scaled[at], basis_refs[at][0], (((1,), (1,)), ((), ())), preferred_element_type=jnp.float32
        ).astype(jnp.bfloat16)


def rotate(slots, grads, inverse, bases):
    matrices, row_count, col_count = grads.shape
    block_count = col_count // BLK
    group = 2 if block_count % 2 == 0 else 1
    steps = block_count // group

    def panel_map(i, slot):
        return i // steps, 0, i % steps

    def slot_map(at, i, slot):
        return slot[i * group + at], 0, 0

    panel = pl.BlockSpec((1, row_count, group * BLK), panel_map)
    return pl.pallas_call(
        functools.partial(rotate_kernel, group),
        grid_spec=pltpu.PrefetchScalarGridSpec(
            num_scalar_prefetch=1,
            grid=(matrices * steps,),
            in_specs=[panel]
            + [pl.BlockSpec((1, 1, BLK), functools.partial(slot_map, at)) for at in range(group)]
            + [pl.BlockSpec((1, BLK, BLK), functools.partial(slot_map, at)) for at in range(group)],
            out_specs=panel,
        ),
        out_shape=jax.ShapeDtypeStruct(grads.shape, grads.dtype),
        compiler_params=pltpu.CompilerParams(vmem_limit_bytes=VMEM_LIMIT),
        cost_estimate=pl.CostEstimate(
            flops=4 * matrices * row_count * col_count * BLK,
            bytes_accessed=4 * matrices * row_count * col_count + 2 * matrices * col_count * BLK,
            transcendentals=0,
        ),
        name="rotate",
    )(slots, grads, *[inverse] * group, *[bases] * group)


def per_device(grads, assign, bases, eigvals):
    owner_count = lax.axis_size("owner")
    owner_here = lax.axis_index("owner")
    matrices, _, col_count = grads.shape
    unit_count = matrices * col_count // BLK
    slot_count = bases.shape[1]
    per_peer = slot_count // owner_count

    units = jnp.arange(unit_count, dtype=jnp.int32)
    owners = lax.dynamic_slice_in_dim(assign[:, 0], owner_here * unit_count, unit_count)
    earlier = units[None, :] < units[:, None]
    ranks = jnp.sum((owners[None, :] == owners[:, None]) & earlier, axis=1, dtype=jnp.int32)
    slots = owners * per_peer + ranks

    inverse = 1.0 / (eigvals[0].astype(jnp.float32) + DAMPING)
    full, full_inverse = gather(
        bases[0].reshape((owner_count, per_peer) + bases.shape[2:]),
        inverse.reshape(owner_count, per_peer, 1, BLK),
    )
    return rotate(
        slots, grads, full_inverse.reshape(slot_count, 1, BLK), full.reshape(slot_count, BLK, BLK)
    )


def solution(mesh):
    in_specs = (
        P("owner", "fsdp", None),
        P(),
        P("owner", None, "fsdp", None),
        P("owner", None, None),
    )
    out_specs = P("owner", "fsdp", None)
    return jax.shard_map(
        per_device, mesh=mesh, in_specs=in_specs, out_specs=out_specs, check_vma=False
    )
```

```python
import functools
import jax
import jax.numpy as jnp
from jax import lax
from jax.experimental import pallas as pl
from jax.experimental.pallas import tpu as pltpu
from jax.sharding import PartitionSpec as P

BLK = 512
DAMPING = 0.1
LAG = 8
WINDOW = 6
MESH = pl.DeviceIdType.MESH
VMEM_LIMIT = 60 * 1024 * 1024


def gather_kernel(
    owners, shards, per_peer,
    bases_ref, inverse_ref, full_ref, full_inverse_ref,
    own_sem, own_inverse_sem, move_send, move_recv, inverse_send, inverse_recv,
    row_send, row_recv, core_send, core_recv,
):
    me, shard = lax.axis_index("owner"), lax.axis_index("fsdp")
    chips = shards // 2
    chip, core = shard // 2, shard % 2
    sibling = chip * 2 + (1 - core)
    pieces = owners * per_peer

    def to(dst_shard, dst_owner):
        return (dst_shard, dst_owner)

    barrier = pltpu.get_barrier_semaphore()
    for step in range(1, owners):
        pl.semaphore_signal(barrier, inc=1, device_id=to(shard, (me + step) % owners), device_id_type=MESH)
    for step in range(1, chips):
        pl.semaphore_signal(barrier, inc=1, device_id=to((chip + step) % chips * 2 + core, me), device_id_type=MESH)
    pl.semaphore_signal(barrier, inc=1, device_id=to(sibling, me), device_id_type=MESH)
    pl.semaphore_wait(barrier, owners - 1 + chips)

    def place(index):
        return index // owners, index % owners

    def partner(turn):
        across_bits = turn % 2 * (owners // 2) + turn // 2
        other, bit = 0, 1
        while bit < owners:
            other = other + (me // bit % 2 + across_bits // bit % 2) % 2 * bit
            bit *= 2
        return other

    def move(index):
        rank, turn = place(index)
        target = partner(turn)
        return pltpu.make_async_remote_copy(
            src_ref=bases_ref.at[target, rank],
            dst_ref=full_ref.at[me, rank, shard],
            send_sem=move_send.at[index],
            recv_sem=move_recv.at[index],
            device_id=to(shard, target),
            device_id_type=MESH,
        )

    def move_inverse(turn):
        target = partner(turn)
        return pltpu.make_async_remote_copy(
            src_ref=inverse_ref.at[target],
            dst_ref=full_inverse_ref.at[me],
            send_sem=inverse_send.at[turn],
            recv_sem=inverse_recv.at[turn],
            device_id=to(shard, target),
            device_id_type=MESH,
        )

    def piece(index, shard_of):
        rank, turn = place(index)
        return full_ref.at[partner(turn), rank, shard_of]

    def along_x(index, step):
        ref = piece(index, shard)
        return pltpu.make_async_remote_copy(
            src_ref=ref, dst_ref=ref,
            send_sem=row_send.at[step - 1, index],
            recv_sem=row_recv.at[step - 1, index],
            device_id=to((chip + step) % chips * 2 + core, me),
            device_id_type=MESH,
        )

    def across(index, step):
        ref = piece(index, (chip + chips - step) % chips * 2 + core)
        return pltpu.make_async_remote_copy(
            src_ref=ref, dst_ref=ref,
            send_sem=core_send.at[step, index],
            recv_sem=core_recv.at[step, index],
            device_id=to(sibling, me),
            device_id_type=MESH,
        )

    def own(rank):
        return pltpu.make_async_copy(bases_ref.at[me, rank], full_ref.at[me, rank, shard], own_sem.at[rank])

    own_inverse = pltpu.make_async_copy(inverse_ref.at[me], full_inverse_ref.at[me], own_inverse_sem)

    for rank in range(per_peer):
        own(rank).start()

    @pl.loop(1, 1 + WINDOW)
    def _(index):
        move(index).start()

    own_inverse.start()

    @pl.loop(1, owners)
    def _(turn):
        move_inverse(turn).start()

    for rank in range(per_peer):
        own(rank).wait()

    def pass_on(index):
        for step in range(1, chips):
            along_x(index, step).wait_recv()
            across(index, step).start()

    @pl.loop(0, pieces)
    def _(index):
        @pl.when(index % owners > 0)
        def _():
            move(index).wait_recv()

        for step in range(1, chips):
            along_x(index, step).start()
        across(index, 0).start()
        later = index + 1 + WINDOW

        @pl.when((later < pieces) & (later % owners > 0))
        def _():
            move(later).start()

        @pl.when(index >= LAG)
        def _():
            pass_on(index - LAG)

    @pl.loop(pieces - LAG, pieces)
    def _(index):
        pass_on(index)

    own_inverse.wait()

    @pl.loop(1, owners)
    def _(turn):
        move_inverse(turn).wait()

    @pl.loop(0, pieces)
    def _(index):
        @pl.when(index % owners > 0)
        def _():
            move(index).wait_send()

        for step in range(1, chips):
            along_x(index, step).wait_send()
        for step in range(chips):
            across(index, step).wait()


def gather(bases, inverse):
    owners, shards = lax.axis_size("owner"), lax.axis_size("fsdp")
    per_peer = bases.shape[1]
    pieces, chips = owners * per_peer, shards // 2
    dma = pltpu.SemaphoreType.DMA
    anywhere = pl.BlockSpec(memory_space=pl.ANY)
    return pl.pallas_call(
        functools.partial(gather_kernel, owners, shards, per_peer),
        out_shape=(
            jax.ShapeDtypeStruct(bases.shape[:2] + (shards,) + bases.shape[2:], bases.dtype),
            jax.ShapeDtypeStruct(inverse.shape, inverse.dtype),
        ),
        in_specs=[anywhere, anywhere],
        out_specs=(anywhere, anywhere),
        scratch_shapes=[
            dma((per_peer,)), dma,
            dma((pieces,)), dma((pieces,)),
            dma((owners,)), dma((owners,)),
            dma((chips - 1, pieces)), dma((chips - 1, pieces)),
            dma((chips, pieces)), dma((chips, pieces)),
        ],
        compiler_params=pltpu.CompilerParams(
            collective_id=0, has_side_effects=True, vmem_limit_bytes=VMEM_LIMIT
        ),
        name="gather",
    )(bases, inverse)


def rotate_kernel(group, slot_ref, panel_ref, *refs):
    inverse_refs, basis_refs, out_ref = refs[:group], refs[group : 2 * group], refs[-1]
    scaled = []
    for at in range(group):
        panel = panel_ref[0, :, at * BLK : (at + 1) * BLK]
        turned = jnp.dot(panel, basis_refs[at][0], preferred_element_type=jnp.float32)
        scaled.append((turned * inverse_refs[at][0]).astype(jnp.bfloat16))
    for at in range(group):
        out_ref[0, :, at * BLK : (at + 1) * BLK] = lax.dot_general(
            scaled[at], basis_refs[at][0], (((1,), (1,)), ((), ())), preferred_element_type=jnp.float32
        ).astype(jnp.bfloat16)


def rotate(slots, grads, inverse, bases):
    matrices, row_count, col_count = grads.shape
    block_count = col_count // BLK
    group = 5 if block_count % 5 == 0 else 1
    steps = block_count // group

    def panel_map(i, slot):
        return i // steps, 0, i % steps

    def slot_map(at, i, slot):
        return slot[i * group + at], 0, 0

    panel = pl.BlockSpec((1, row_count, group * BLK), panel_map)
    return pl.pallas_call(
        functools.partial(rotate_kernel, group),
        grid_spec=pltpu.PrefetchScalarGridSpec(
            num_scalar_prefetch=1,
            grid=(matrices * steps,),
            in_specs=[panel]
            + [pl.BlockSpec((1, 1, BLK), functools.partial(slot_map, at)) for at in range(group)]
            + [pl.BlockSpec((1, BLK, BLK), functools.partial(slot_map, at)) for at in range(group)],
            out_specs=panel,
        ),
        out_shape=jax.ShapeDtypeStruct(grads.shape, grads.dtype),
        compiler_params=pltpu.CompilerParams(vmem_limit_bytes=VMEM_LIMIT),
        cost_estimate=pl.CostEstimate(
            flops=4 * matrices * row_count * col_count * BLK,
            bytes_accessed=4 * matrices * row_count * col_count + 2 * matrices * col_count * BLK,
            transcendentals=0,
        ),
        name="rotate",
    )(slots, grads, *[inverse] * group, *[bases] * group)


def per_device(grads, assign, bases, eigvals):
    owner_count = lax.axis_size("owner")
    owner_here = lax.axis_index("owner")
    matrices, _, col_count = grads.shape
    unit_count = matrices * col_count // BLK
    slot_count = bases.shape[1]
    per_peer = slot_count // owner_count

    units = jnp.arange(unit_count, dtype=jnp.int32)
    owners = lax.dynamic_slice_in_dim(assign[:, 0], owner_here * unit_count, unit_count)
    earlier = units[None, :] < units[:, None]
    ranks = jnp.sum((owners[None, :] == owners[:, None]) & earlier, axis=1, dtype=jnp.int32)
    slots = owners * per_peer + ranks

    inverse = 1.0 / (eigvals[0].astype(jnp.float32) + DAMPING)
    full, full_inverse = gather(
        bases[0].reshape((owner_count, per_peer) + bases.shape[2:]),
        inverse.reshape(owner_count, per_peer, 1, BLK),
    )
    return rotate(
        slots, grads, full_inverse.reshape(slot_count, 1, BLK), full.reshape(slot_count, BLK, BLK)
    )


def solution(mesh):
    in_specs = (
        P("owner", "fsdp", None),
        P(),
        P("owner", None, "fsdp", None),
        P("owner", None, None),
    )
    out_specs = P("owner", "fsdp", None)
    return jax.shard_map(
        per_device, mesh=mesh, in_specs=in_specs, out_specs=out_specs, check_vma=False
    )
```
